32 devices in a mesh: grp: 4 (over y, core), fsdp: 8 (over z, x).
Axes of the slice: x: 2, y: 2, z: 4, core: 2. Of those that a mesh axis runs over, the one named last changes fastest.
Arguments:
- patches: bfloat16 [128, 196, 768], P(('grp', 'fsdp')), may hold values from -6 to 6
- positions: int32 [128, 75], P(('grp', 'fsdp')), may hold values from 1 to 196, as said below
- codes: int32 [128, 75], P(('grp', 'fsdp')), may hold values from 0 to 8191
- owners: int32 [8], replicated, may hold values from 0 to 3
- bases: float32 [8, 768, 768], replicated, as said below
- patch_weight: float32 [768, 768], P(None, 'fsdp'), may hold values from -0.21875 to 0.21875
- head_weight: float32 [768, 8192], P(None, 'fsdp'), may hold values from -0.21875 to 0.21875
- vocab_bias: float32 [8192], P('fsdp'), may hold values from -3 to 3
- token_vectors: float32 [5, 768], replicated
- qkv_weight: float32 [2, 768, 2304], P(None, None, 'fsdp'), may hold values from -0.21875 to 0.21875
- out_weight: float32 [2, 768, 768], P(None, None, 'fsdp'), may hold values from -0.625 to 0.625
- up_weight: float32 [2, 768, 3072], P(None, None, 'fsdp'), may hold values from -0.21875 to 0.21875
- down_weight: float32 [2, 3072, 768], P(None, 'fsdp'), may hold values from -0.109375 to 0.109375
- layer_vectors: float32 [2, 19536], replicated
- first_patch: float32 [768, 768], P(None, 'fsdp'), may hold values from -0.00012207031 to 0.00012207031
- first_head: float32 [768, 8192], P(None, 'fsdp'), may hold values from -0.00012207031 to 0.00012207031
- first_vocab: float32 [8192], P('fsdp'), may hold values from -0.00061035156 to 0.00061035156
- first_token: float32 [5, 768], replicated, may hold values from -0.00061035156 to 0.00061035156
- first_qkv: float32 [2, 768, 2304], P(None, None, 'fsdp'), may hold values from -0.00012207031 to 0.00012207031
- first_out: float32 [2, 768, 768], P(None, None, 'fsdp'), may hold values from -0.00012207031 to 0.00012207031
- first_up: float32 [2, 768, 3072], P(None, None, 'fsdp'), may hold values from -0.00012207031 to 0.00012207031
- first_down: float32 [2, 3072, 768], P(None, 'fsdp'), may hold values from -0.00012207031 to 0.00012207031
- first_layer: float32 [2, 19536], replicated, may hold values from -0.00061035156 to 0.00061035156
- second_patch: float32 [768, 768], P(None, 'fsdp'), may hold values from 4.7419974e-11 to 1.896799e-10
- second_head: float32 [768, 8192], P(None, 'fsdp'), may hold values from 4.7419974e-11 to 1.896799e-10
- second_vocab: float32 [8192], P('fsdp'), may hold values from 1.1854994e-09 to 4.7419975e-09
- second_token: float32 [5, 768], replicated, may hold values from 1.1854994e-09 to 4.7419975e-09
- second_qkv: float32 [2, 768, 2304], P(None, None, 'fsdp'), may hold values from 4.7419974e-11 to 1.896799e-10
- second_out: float32 [2, 768, 768], P(None, None, 'fsdp'), may hold values from 4.7419974e-11 to 1.896799e-10
- second_up: float32 [2, 768, 3072], P(None, None, 'fsdp'), may hold values from 4.7419974e-11 to 1.896799e-10
- second_down: float32 [2, 3072, 768], P(None, 'fsdp'), may hold values from 4.7419974e-11 to 1.896799e-10
- second_layer: float32 [2, 19536], replicated, may hold values from 1.1854994e-09 to 4.7419975e-09
Outputs:
- loss_sum: float32 [], replicated
- clip_norm: float32 [], replicated
- new_patch: float32 [768, 768], P(None, 'fsdp')
- new_head: float32 [768, 8192], P(None, 'fsdp')
- new_vocab: float32 [8192], P('fsdp')
- new_token: float32 [5, 768], replicated
- new_qkv: float32 [2, 768, 2304], P(None, None, 'fsdp')
- new_out: float32 [2, 768, 768], P(None, None, 'fsdp')
- new_up: float32 [2, 768, 3072], P(None, None, 'fsdp')
- new_down: float32 [2, 3072, 768], P(None, 'fsdp')
- new_layer: float32 [2, 19536], replicated
- moment_patch: float32 [768, 768], P(None, 'fsdp')
- moment_head: float32 [768, 8192], P(None, 'fsdp')
- moment_vocab: float32 [8192], P('fsdp')
- moment_token: float32 [5, 768], replicated
- moment_qkv: float32 [2, 768, 2304], P(None, None, 'fsdp')
- moment_out: float32 [2, 768, 768], P(None, None, 'fsdp')
- moment_up: float32 [2, 768, 3072], P(None, None, 'fsdp')
- moment_down: float32 [2, 3072, 768], P(None, 'fsdp')
- moment_layer: float32 [2, 19536], replicated
- square_patch: float32 [768, 768], P(None, 'fsdp')
- square_head: float32 [768, 8192], P(None, 'fsdp')
- square_vocab: float32 [8192], P('fsdp')
- square_token: float32 [5, 768], replicated
- square_qkv: float32 [2, 768, 2304], P(None, None, 'fsdp')
- square_out: float32 [2, 768, 768], P(None, None, 'fsdp')
- square_up: float32 [2, 768, 3072], P(None, None, 'fsdp')
- square_down: float32 [2, 3072, 768], P(None, 'fsdp')
- square_layer: float32 [2, 19536], replicated
The draws below stay inside these ranges and needn't reach their ends.
Inputs may be any that keep to these rules, and one draw needn't show every extreme that they name: The 75 positions of an image are distinct token indices of patches. `bases`: each basis is orthogonal.
All inputs are finite; a program needn't handle non-finite values.
Results may differ from the reference program's by a relative error of at most 0.018.
Values may be sent and summed in bfloat16 or wider, within the bound.
A program may use at most 448 MiB of HBM per device.

```python
import math
import jax
import jax.numpy as jnp
import numpy as np
from jax import lax

D = 768
H = 12
HD = 64
FF = 3072
V = 8192
PIX = 768
SIDE = 14
L = 2
NMASK = 75
STEP = 10
NPATCH = 196
NREL = 732
VW = 19536
IMAGES = 128
NPARAM = 21088160
N_GRP = 4


def draw_positions(key, part):
    key = jax.random.fold_in(key, 1)
    keys = jax.random.split(key, IMAGES)
    picked = jax.vmap(lambda item_key: jax.random.permutation(item_key, NPATCH)[:NMASK])(keys)
    return (picked + 1).astype(jnp.int32)


def draw_bases(key, part):
    key = jax.random.fold_in(key, 2)
    angle_key, vector_key = jax.random.split(key)
    count = L * 4
    angles = jax.random.uniform(angle_key, (count, D // 2), jnp.float32, -3.14159, 3.14159)
    cosine = jnp.repeat(jnp.cos(angles), 2, axis=1)
    sine = jnp.repeat(jnp.sin(angles), 2, axis=1)
    places = jnp.arange(D)
    signed = jnp.where(places[None, :] % 2 == 0, -sine, sine)
    partner_index = places ^ 1
    row_ids = places[:, None]
    col_ids = places[None, :]
    diagonal = jnp.where(row_ids == col_ids, cosine[:, :, None], 0.0)
    partner = jnp.where(col_ids == row_ids ^ 1, signed[:, :, None], 0.0)
    rotation = diagonal + partner
    vectors = jax.random.normal(vector_key, (count, D), jnp.float32)
    lengths = jnp.sum(vectors * vectors, axis=1)
    mixed = vectors * cosine + vectors[:, partner_index] * signed[:, partner_index]
    return rotation - 2.0 * vectors[:, :, None] * mixed[:, None, :] / lengths[:, None, None]


def draw_token_vectors(key, part):
    key = jax.random.fold_in(key, 3)
    keys = jax.random.split(key, 5)
    embed_bias = 0.3 * jax.random.normal(keys[0], (D,), jnp.float32)
    leading = jax.random.normal(keys[1], (D,), jnp.float32)
    mask_token = jax.random.normal(keys[2], (D,), jnp.float32)
    final_gain = jax.random.uniform(keys[3], (D,), jnp.float32, 0.7, 1.3)
    final_bias = 0.3 * jax.random.normal(keys[4], (D,), jnp.float32)
    return jnp.stack([embed_bias, leading, mask_token, final_gain, final_bias])


def draw_layer_vectors(key, part):
    key = jax.random.fold_in(key, 4)
    keys = jax.random.split(key, 5)
    gains = jax.random.uniform(keys[0], (L, 2, D), jnp.float32, 0.7, 1.3)
    biases = 0.2 * jax.random.normal(keys[1], (L, 6, D), jnp.float32)
    scales = jnp.exp(jax.random.uniform(keys[2], (L, 2, D), jnp.float32, -1.2, 0.0))
    fc_bias = 0.2 * jax.random.normal(keys[3], (L, FF), jnp.float32)
    tables = jax.random.normal(keys[4], (L, H * NREL), jnp.float32)
    pieces = [gains[:, 0], biases[:, 0], biases[:, 1], biases[:, 2], biases[:, 3], scales[:, 0], gains[:, 1], biases[:, 4], biases[:, 5], scales[:, 1], fc_bias, tables]
    return jnp.concatenate(pieces, axis=1)


def set_ends(values, own_key, low, high):
    place = [jax.random.randint(jax.random.fold_in(own_key, axis), (), 0, length) for axis, length in enumerate(values.shape)]
    longest = values.shape.index(max(values.shape))
    next_to = place[:longest] + [(place[longest] + 1) % values.shape[longest]] + place[longest + 1:]
    return values.at[tuple(place)].set(low).at[tuple(next_to)].set(high)


def block_levels(own_key, extent, cuts, low, high):
    def one(axis_at, blocks):
        heights = jax.random.uniform(jax.random.fold_in(jax.random.fold_in(own_key, 6), axis_at), (blocks,), jnp.float32, low / len(cuts), high / len(cuts))
        return jnp.repeat(jnp.exp(heights), extent[axis_at] // blocks).reshape((-1,) + (1,) * (len(extent) - axis_at - 1))

    level = one(*cuts[0])
    for cut in cuts[1:]:
        level = level * one(*cut)
    return level


def bell_draw(own_key, dims, deviation, bound, shards=(), kind=jnp.bfloat16):
    values = deviation * jax.random.normal(own_key, dims, jnp.float32)
    if shards:
        values = values * block_levels(own_key, dims, shards, -0.22, 0.18)
    return jnp.clip(values, -bound, bound).astype(kind)


def setup_inputs(seed: int = 0) -> dict:
    streams_of = jax.random.split(jax.random.key(seed), 33)
    patches = bell_draw(streams_of[0], (IMAGES, NPATCH, PIX), 1.0, 6.0, ((0, 32),))
    positions = draw_positions(jax.random.fold_in(streams_of[32], 71), 0)
    codes = set_ends(jax.random.randint(streams_of[2], (IMAGES, NMASK), 0, V), jax.random.fold_in(streams_of[2], 1), 0, V - 1).astype(jnp.int32)
    owners = set_ends(jax.random.randint(streams_of[3], (4 * L,), 0, N_GRP), jax.random.fold_in(streams_of[3], 1), 0, N_GRP - 1).astype(jnp.int32)
    bases = draw_bases(jax.random.fold_in(streams_of[32], 71), 0)
    patch_weight = bell_draw(streams_of[5], (PIX, D), PIX ** -0.5, 0.21875, ((1, 8),), jnp.float32)
    head_weight = bell_draw(streams_of[6], (D, V), D ** -0.5, 0.21875, ((1, 8),), jnp.float32)
    vocab_bias = bell_draw(streams_of[7], (V,), 0.5, 3.0, ((0, 8),), jnp.float32)
    token_vectors = draw_token_vectors(jax.random.fold_in(streams_of[32], 71), 0)
    qkv_weight = bell_draw(streams_of[9], (L, D, 3 * D), D ** -0.5, 0.21875, ((2, 8),), jnp.float32)
    out_weight = bell_draw(streams_of[10], (L, D, D), (D // 8) ** -0.5, 0.625, ((2, 8),), jnp.float32)
    up_weight = bell_draw(streams_of[11], (L, D, FF), D ** -0.5, 0.21875, ((2, 8),), jnp.float32)
    down_weight = bell_draw(streams_of[12], (L, FF, D), FF ** -0.5, 0.109375, ((1, 8),), jnp.float32)
    layer_vectors = draw_layer_vectors(jax.random.fold_in(streams_of[32], 71), 0)
    first_patch = bell_draw(streams_of[14], (PIX, D), (0.1 / NPARAM ** 0.5), 0.00012207031, ((1, 8),), jnp.float32)
    first_head = bell_draw(streams_of[15], (D, V), (0.1 / NPARAM ** 0.5), 0.00012207031, ((1, 8),), jnp.float32)
    first_vocab = bell_draw(streams_of[16], (V,), (0.5 / NPARAM ** 0.5), 0.00061035156, ((0, 8),), jnp.float32)
    first_token = bell_draw(streams_of[17], (5, D), (0.5 / NPARAM ** 0.5), 0.00061035156, (), jnp.float32)
    first_qkv = bell_draw(streams_of[18], (L, D, 3 * D), (0.1 / NPARAM ** 0.5), 0.00012207031, ((2, 8),), jnp.float32)
    first_out = bell_draw(streams_of[19], (L, D, D), (0.1 / NPARAM ** 0.5), 0.00012207031, ((2, 8),), jnp.float32)
    first_up = bell_draw(streams_of[20], (L, D, FF), (0.1 / NPARAM ** 0.5), 0.00012207031, ((2, 8),), jnp.float32)
    first_down = bell_draw(streams_of[21], (L, FF, D), (0.1 / NPARAM ** 0.5), 0.00012207031, ((1, 8),), jnp.float32)
    first_layer = bell_draw(streams_of[22], (L, VW), (0.5 / NPARAM ** 0.5), 0.00061035156, (), jnp.float32)
    second_patch = jnp.clip(jnp.exp(math.log(1.8967989678930763e-10) - 1.3862944 * jax.random.uniform(streams_of[23], (PIX, D), jnp.float32) ** block_levels(streams_of[23], (PIX, D), ((1, 8),), -0.2, 0.2)), 4.741997419732691e-11, 1.8967989678930763e-10)
    second_head = jnp.clip(jnp.exp(math.log(1.8967989678930763e-10) - 1.3862944 * jax.random.uniform(streams_of[24], (D, V), jnp.float32) ** block_levels(streams_of[24], (D, V), ((1, 8),), -0.2, 0.2)), 4.741997419732691e-11, 1.8967989678930763e-10)
    second_vocab = jnp.clip(jnp.exp(math.log(4.741997461366054e-09) - 1.3862944 * jax.random.uniform(streams_of[25], (V,), jnp.float32) ** block_levels(streams_of[25], (V,), ((0, 8),), -0.2, 0.2)), 1.1854993653415136e-09, 4.741997461366054e-09)
    second_token = jnp.clip(jnp.exp(jax.random.uniform(streams_of[26], (5, D), jnp.float32, math.log(1.1854993653415136e-09), math.log(4.741997461366054e-09))), 1.1854993653415136e-09, 4.741997461366054e-09)
    second_qkv = jnp.clip(jnp.exp(math.log(1.8967989678930763e-10) - 1.3862944 * jax.random.uniform(streams_of[27], (L, D, 3 * D), jnp.float32) ** block_levels(streams_of[27], (L, D, 3 * D), ((2, 8),), -0.2, 0.2)), 4.741997419732691e-11, 1.8967989678930763e-10)
    second_out = jnp.clip(jnp.exp(math.log(1.8967989678930763e-10) - 1.3862944 * jax.random.uniform(streams_of[28], (L, D, D), jnp.float32) ** block_levels(streams_of[28], (L, D, D), ((2, 8),), -0.2, 0.2)), 4.741997419732691e-11, 1.8967989678930763e-10)
    second_up = jnp.clip(jnp.exp(math.log(1.8967989678930763e-10) - 1.3862944 * jax.random.uniform(streams_of[29], (L, D, FF), jnp.float32) ** block_levels(streams_of[29], (L, D, FF), ((2, 8),), -0.2, 0.2)), 4.741997419732691e-11, 1.8967989678930763e-10)
    second_down = jnp.clip(jnp.exp(math.log(1.8967989678930763e-10) - 1.3862944 * jax.random.uniform(streams_of[30], (L, FF, D), jnp.float32) ** block_levels(streams_of[30], (L, FF, D), ((1, 8),), -0.2, 0.2)), 4.741997419732691e-11, 1.8967989678930763e-10)
    second_layer = jnp.clip(jnp.exp(jax.random.uniform(streams_of[31], (L, VW), jnp.float32, math.log(1.1854993653415136e-09), math.log(4.741997461366054e-09))), 1.1854993653415136e-09, 4.741997461366054e-09)
    return dict(patches=patches, positions=positions, codes=codes, owners=owners, bases=bases, patch_weight=patch_weight, head_weight=head_weight, vocab_bias=vocab_bias, token_vectors=token_vectors, qkv_weight=qkv_weight, out_weight=out_weight, up_weight=up_weight, down_weight=down_weight, layer_vectors=layer_vectors, first_patch=first_patch, first_head=first_head, first_vocab=first_vocab, first_token=first_token, first_qkv=first_qkv, first_out=first_out, first_up=first_up, first_down=first_down, first_layer=first_layer, second_patch=second_patch, second_head=second_head, second_vocab=second_vocab, second_token=second_token, second_qkv=second_qkv, second_out=second_out, second_up=second_up, second_down=second_down, second_layer=second_layer)


@jax.custom_vjp
def low(v):
    return lax.optimization_barrier(v.astype(jnp.bfloat16)).astype(jnp.float32)

@jax.custom_vjp
def low_back(v):
    return v

def low_keep(v):
    return (low(v), None)

def low_pass(kept, grad):
    return (grad,)

def back_keep(v):
    return (v, None)

def back_low(kept, grad):
    return (low(grad),)
low.defvjp(low_keep, low_pass)
low_back.defvjp(back_keep, back_low)
highest = lax.Precision.HIGHEST
beta_one = 0.9
beta_two = 0.999
adam_eps = 1e-08
matrix_rate = 0.06
vector_rate = 0.5
weight_decay = 0.05
clip_level = 1.0
norm_eps = 1e-06

def product(left_side, right_side):
    return jnp.dot(left_side, right_side, precision=highest, preferred_element_type=jnp.float32)

def relative_index(side):
    coords = np.stack(np.meshgrid(np.arange(side), np.arange(side), indexing='ij')).reshape(2, -1)
    offsets = coords[:, :, None] - coords[:, None, :] + side - 1
    inner = offsets[0] * (2 * side - 1) + offsets[1]
    far_count = (2 * side - 1) ** 2
    index_table = np.full((side * side + 1, side * side + 1), far_count + 2, dtype=np.int32)
    index_table[1:, 1:] = inner
    index_table[0, 1:] = far_count
    index_table[1:, 0] = far_count + 1
    return jnp.asarray(index_table)

def layer_norm(values, gain_row, bias_row):
    centered = values - lax.optimization_barrier(jnp.mean(values, axis=-1, keepdims=True))
    spread = lax.optimization_barrier(jnp.mean(centered * centered, axis=-1, keepdims=True))
    return centered * lax.rsqrt(spread + norm_eps) * gain_row + bias_row

def unpack(vectors):
    pieces = [vectors[slot * D:(slot + 1) * D] for slot in range(10)]
    fc_bias = vectors[10 * D:10 * D + FF]
    bias_table = vectors[10 * D + FF:].reshape(H, NREL)
    return (pieces, fc_bias, bias_table)

def layer(states, qkv_weight, out_weight, up_weight, down_weight, vectors):
    pieces, fc_bias, bias_table = unpack(vectors)
    gain_one, bias_one, query_bias, value_bias, out_bias, scale_one, gain_two, bias_two, down_bias, scale_two = pieces
    count, length = (states.shape[0], states.shape[1])
    normed = low(layer_norm(states, gain_one, bias_one))
    qkv_bias = jnp.concatenate([query_bias, jnp.zeros_like(query_bias), value_bias])
    projected = low(low_back(product(normed, low(qkv_weight)) + qkv_bias)).reshape(count, length, 3, H, HD)
    scores = low_back(jnp.einsum('nqhd,nkhd->nhqk', projected[:, :, 0], projected[:, :, 1], precision=highest))
    position_bias = jnp.take(bias_table, relative_index(SIDE), axis=1)
    scores = scores * HD ** (-0.5) + position_bias[None]
    attention = low(jax.nn.softmax(scores, axis=-1))
    attended = low(low_back(jnp.einsum('nhqk,nkhd->nqhd', attention, projected[:, :, 2], precision=highest)))
    attended = attended.reshape(count, length, D)
    states = states + scale_one * low_back(product(attended, low(out_weight)) + out_bias)
    normed_two = low(layer_norm(states, gain_two, bias_two))
    hidden = low(jax.nn.gelu(low_back(product(normed_two, low(up_weight)) + fc_bias), approximate=False))
    return states + scale_two * low_back(product(hidden, low(down_weight)) + down_bias)

def patch_mask(positions):
    slots = jnp.arange(1, NPATCH + 1, dtype=jnp.int32)
    return lax.optimization_barrier(jnp.sum((positions[:, :, None] == slots[None, None, :]).astype(jnp.float32), axis=1))

def embed(patches, patch_weight, token_vectors, masked):
    tokens = low_back(product(low(patches), low(patch_weight)) + token_vectors[0])
    tokens = tokens * (1.0 - masked[..., None]) + token_vectors[2] * masked[..., None]
    leading = jnp.broadcast_to(token_vectors[1], (tokens.shape[0], 1, D))
    return jnp.concatenate([leading, tokens], axis=1)

def final_rows(states, token_vectors, positions):
    normed = layer_norm(states, token_vectors[3], token_vectors[4])
    return low(jnp.take_along_axis(normed, positions[:, :, None], axis=1))

def adam_step(weight, grad, first_moment, second_moment, decay, rate):
    first_moment = beta_one * first_moment + (1 - beta_one) * grad
    second_moment = beta_two * second_moment + (1 - beta_two) * grad * grad
    update = first_moment / (1 - beta_one ** STEP) / (jnp.sqrt(second_moment / (1 - beta_two ** STEP)) + adam_eps)
    return (weight - rate * (update + decay * weight), first_moment, second_moment)

def rotated_step(weight, grad, first_moment, second_moment, basis, on_left):
    turned = product(basis.T, grad) if on_left else product(grad, basis)
    first_moment = beta_one * first_moment + (1 - beta_one) * turned
    second_moment = beta_two * second_moment + (1 - beta_two) * turned * turned
    update = first_moment / (1 - beta_one ** STEP) / (jnp.sqrt(second_moment / (1 - beta_two ** STEP)) + adam_eps)
    update = product(basis, update) if on_left else product(update, basis.T)
    return (weight - matrix_rate * (update + weight_decay * weight), first_moment, second_moment)

def forward(patches, positions, codes, patch_weight, head_weight, vocab_bias, token_vectors, qkv_weight, out_weight, up_weight, down_weight, layer_vectors):
    group_size = 16

    def one_group(running, inputs):
        patch_group, position_group, code_group = inputs
        states = embed(patch_group, patch_weight, token_vectors, patch_mask(position_group))
        for layer_index in range(L):
            states = layer(states, qkv_weight[layer_index], out_weight[layer_index], up_weight[layer_index], down_weight[layer_index], layer_vectors[layer_index])
        rows = final_rows(states, token_vectors, position_group).reshape(-1, D)
        logits = low_back(product(rows, low(head_weight))) + vocab_bias
        target = jnp.take_along_axis(logits, code_group.reshape(-1, 1), axis=1)[:, 0]
        return (running + jnp.sum(jax.nn.logsumexp(logits, axis=-1) - target), None)
    inputs = (patches.reshape(-1, group_size, NPATCH, PIX), positions.reshape(-1, group_size, NMASK), codes.reshape(-1, group_size, NMASK))
    loss_sum, unused = lax.scan(jax.checkpoint(one_group), jnp.zeros((), jnp.float32), inputs)
    return loss_sum

def reference(patches, positions, codes, owners, bases, patch_weight, head_weight, vocab_bias, token_vectors, qkv_weight, out_weight, up_weight, down_weight, layer_vectors, first_patch, first_head, first_vocab, first_token, first_qkv, first_out, first_up, first_down, first_layer, second_patch, second_head, second_vocab, second_token, second_qkv, second_out, second_up, second_down, second_layer):
    weights = (patch_weight, head_weight, vocab_bias, token_vectors, qkv_weight, out_weight, up_weight, down_weight, layer_vectors)
    firsts = (first_patch, first_head, first_vocab, first_token, first_qkv, first_out, first_up, first_down, first_layer)
    seconds = (second_patch, second_head, second_vocab, second_token, second_qkv, second_out, second_up, second_down, second_layer)
    patch_values = patches.astype(jnp.float32)

    def objective(*params):
        return forward(patch_values, positions, codes, *params)
    loss_sum, pull = jax.vjp(objective, *weights)
    grads = pull(jnp.ones((), jnp.float32))
    squares = jnp.zeros((), jnp.float32)
    for grad in grads:
        squares = squares + jnp.sum(grad * grad)
    clip_norm = jnp.sqrt(squares)
    clip_scale = jnp.minimum(1.0, clip_level / (clip_norm + 1e-06))
    decays = (weight_decay, weight_decay, 0.0, 0.0)
    rates = (matrix_rate, matrix_rate, vector_rate, vector_rate)
    updates = [adam_step(weights[slot], grads[slot] * clip_scale, firsts[slot], seconds[slot], decays[slot], rates[slot]) for slot in range(4)]
    for matrix_kind in range(4):
        slot = 4 + matrix_kind
        results = [rotated_step(weights[slot][layer_index], grads[slot][layer_index] * clip_scale, firsts[slot][layer_index], seconds[slot][layer_index], bases[4 * layer_index + matrix_kind], matrix_kind < 3) for layer_index in range(L)]
        updates.append(tuple((jnp.stack([result[member] for result in results]) for member in range(3))))
    updates.append(adam_step(layer_vectors, grads[8] * clip_scale, first_layer, second_layer, 0.0, vector_rate))
    return (loss_sum, clip_norm, *[entry[0] for entry in updates], *[entry[1] for entry in updates], *[entry[2] for entry in updates])
```

```python
import functools

import jax
import jax.numpy as jnp
from jax import lax
from jax.experimental import pallas as pl
from jax.experimental.pallas import tpu as pltpu
from jax.sharding import PartitionSpec as P

D = 768
H = 12
HD = 64
FF = 3072
SIDE = 14
SPAN = 2 * SIDE - 1
FAR = SPAN * SPAN
NMASK = 75
STEP = 10
NPATCH = 196
NREL = 732
TOK = 208
STRIP = 384
RELPAD = 736

beta_one = 0.9
beta_two = 0.999
adam_eps = 1e-08
matrix_rate = 0.06
vector_rate = 0.5
weight_decay = 0.05
clip_level = 1.0
norm_eps = 1e-06

BF = jnp.bfloat16
F32 = jnp.float32
NN = (((1,), (0,)), ((), ()))
NT = (((1,), (1,)), ((), ()))
TN = (((0,), (0,)), ((), ()))


def dot(a, b, dims=NN):
    return lax.dot_general(a, b, dims, preferred_element_type=F32)


def three_parts(value):
    high = value.astype(BF)
    rest = value - high.astype(F32)
    middle = rest.astype(BF)
    return high, middle, (rest - middle.astype(F32)).astype(BF)


def one_hot_strip(xa):
    slot = lax.broadcasted_iota(jnp.int32, (RELPAD, STRIP), 0)
    lane = lax.broadcasted_iota(jnp.int32, (1, STRIP), 1)
    wanted = (SPAN - 1 - lane // SIDE) * SPAN + xa - lane % SIDE + SIDE - 1
    wanted = jnp.where(lane < SPAN * SIDE, wanted, -1)
    return (slot == wanted).astype(BF)


def expand_kernel(table_ref, bias_ref, strip_ref):
    table = table_ref[...]
    parts = jnp.concatenate(three_parts(table), axis=0)
    rows = table.shape[0]
    for xa in range(SIDE):
        got = dot(parts, one_hot_strip(xa))
        strip_ref[:, xa, :] = got[:rows] + got[rows : 2 * rows] + got[2 * rows :]
    row = lax.broadcasted_iota(jnp.int32, (TOK, TOK), 0)
    col = lax.broadcasted_iota(jnp.int32, (TOK, TOK), 1)
    for h in range(H):
        strip = strip_ref[h]
        for ya in range(SIDE):
            start = (SIDE - 1 - ya) * SIDE
            turned = pltpu.roll(strip, (STRIP - start) % STRIP, 1)
            bias_ref[h, ya * SIDE : (ya + 1) * SIDE, :] = turned[:SIDE, :TOK]
        bias_ref[h, NPATCH:TOK, :] = jnp.zeros((TOK - NPATCH, TOK), F32)
        top = table[h : h + 1, FAR : FAR + 1]
        left = table[h : h + 1, FAR + 1 : FAR + 2]
        corner = table[h : h + 1, FAR + 2 : FAR + 3]
        value = bias_ref[h]
        value = jnp.where(row == NPATCH, top, value)
        value = jnp.where(col == NPATCH, jnp.where(row == NPATCH, corner, left), value)
        bias_ref[h] = jnp.where(col > NPATCH, -1e30, value)


def expand_bias(table):
    padded = jnp.pad(table, ((0, 16 - H), (0, RELPAD - NREL)))
    return pl.pallas_call(
        expand_kernel,
        out_shape=jax.ShapeDtypeStruct((H, TOK, TOK), F32),
        in_specs=[pl.BlockSpec(memory_space=pltpu.VMEM)],
        out_specs=pl.BlockSpec(memory_space=pltpu.VMEM),
        scratch_shapes=[pltpu.VMEM((16, 16, STRIP), F32)],
        compiler_params=pltpu.CompilerParams(vmem_limit_bytes=48 << 20),
    )(padded)


def reduce_kernel(grad_ref, table_ref, strip_ref):
    lane = lax.broadcasted_iota(jnp.int32, (SIDE, STRIP), 1)
    row = lax.broadcasted_iota(jnp.int32, (TOK, TOK), 0)
    col = lax.broadcasted_iota(jnp.int32, (TOK, TOK), 1)
    slots = lax.broadcasted_iota(jnp.int32, (1, RELPAD), 1)
    strip_ref[...] = jnp.zeros_like(strip_ref)
    for h in range(H):
        total = jnp.zeros((SIDE, STRIP), F32)
        for ya in range(SIDE):
            start = (SIDE - 1 - ya) * SIDE
            window = grad_ref[h, ya * SIDE : (ya + 1) * SIDE, :]
            window = jnp.concatenate(
                [window, jnp.zeros((SIDE, STRIP - TOK), F32)], axis=1
            )
            window = jnp.where(lane < NPATCH, window, 0.0)
            total = total + pltpu.roll(window, start, 1)
        strip_ref[h, :SIDE, :] = total
    acc = jnp.zeros((16, RELPAD), F32)
    for xa in range(SIDE):
        high, middle, unused = three_parts(strip_ref[:, xa, :])
        got = dot(jnp.concatenate([high, middle], axis=0), one_hot_strip(xa), NT)
        acc = acc + got[:16] + got[16:]
    for h in range(H):
        value = grad_ref[h]
        top = jnp.where((row == NPATCH) & (col < NPATCH), value, 0.0)
        left = jnp.where((col == NPATCH) & (row < NPATCH), value, 0.0)
        corner = jnp.where((col == NPATCH) & (row == NPATCH), value, 0.0)
        extra = jnp.where(slots == FAR, jnp.sum(top, keepdims=True), 0.0)
        extra = extra + jnp.where(slots == FAR + 1, jnp.sum(left, keepdims=True), 0.0)
        extra = extra + jnp.where(slots == FAR + 2, jnp.sum(corner, keepdims=True), 0.0)
        table_ref[h : h + 1, :] = acc[h : h + 1] + extra


def reduce_bias(grad):
    table = pl.pallas_call(
        reduce_kernel,
        out_shape=jax.ShapeDtypeStruct((16, RELPAD), F32),
        in_specs=[pl.BlockSpec(memory_space=pltpu.VMEM)],
        out_specs=pl.BlockSpec(memory_space=pltpu.VMEM),
        scratch_shapes=[pltpu.VMEM((16, 16, STRIP), F32)],
        compiler_params=pltpu.CompilerParams(vmem_limit_bytes=48 << 20),
    )(grad)
    return table[:H, :NREL]


def attend_kernel(qkv_ref, bias_ref, out_ref, prob_ref):
    lane = lax.broadcasted_iota(jnp.int32, (1, 2 * HD), 1)
    for pair in range(H // 2):
        lo = pair * 2 * HD
        query = qkv_ref[:, lo : lo + 2 * HD]
        key = qkv_ref[:, D + lo : D + lo + 2 * HD]
        value = qkv_ref[:, 2 * D + lo : 2 * D + lo + 2 * HD]
        outs = []
        for side in range(2):
            mine = (lane // HD) == side
            scores = dot(jnp.where(mine, query, jnp.zeros_like(query)), key, NT)
            scores = scores * HD**-0.5 + bias_ref[2 * pair + side]
            scores = jnp.exp(scores - jnp.max(scores, axis=1, keepdims=True))
            total = jnp.sum(scores, axis=1, keepdims=True)
            prob = (scores * (1.0 / total)).astype(BF)
            prob_ref[0, 2 * pair + side] = prob
            outs.append(dot(prob, value))
        out_ref[:, lo : lo + 2 * HD] = jnp.where(lane < HD, outs[0], outs[1]).astype(BF)


def attend(qkv, bias):
    count = qkv.shape[0] // TOK
    return pl.pallas_call(
        attend_kernel,
        grid=(count,),
        out_shape=(
            jax.ShapeDtypeStruct((count * TOK, D), BF),
            jax.ShapeDtypeStruct((count, H, TOK, TOK), BF),
        ),
        in_specs=[
            pl.BlockSpec((TOK, 3 * D), lambda i: (i, 0)),
            pl.BlockSpec((H, TOK, TOK), lambda i: (0, 0, 0)),
        ],
        out_specs=(
            pl.BlockSpec((TOK, D), lambda i: (i, 0)),
            pl.BlockSpec((1, H, TOK, TOK), lambda i: (i, 0, 0, 0)),
        ),
        compiler_params=pltpu.CompilerParams(vmem_limit_bytes=48 << 20),
    )(qkv, bias)


def attend_back_kernel(qkv_ref, prob_ref, grad_ref, dqkv_ref, dbias_ref):
    lane = lax.broadcasted_iota(jnp.int32, (1, 2 * HD), 1)

    @pl.when(pl.program_id(0) == 0)
    def clear():
        dbias_ref[...] = jnp.zeros_like(dbias_ref)

    for pair in range(H // 2):
        lo = pair * 2 * HD
        query = qkv_ref[:, lo : lo + 2 * HD]
        key = qkv_ref[:, D + lo : D + lo + 2 * HD]
        value = qkv_ref[:, 2 * D + lo : 2 * D + lo + 2 * HD]
        grad = grad_ref[:, lo : lo + 2 * HD]
        queries, keys, values = [], [], []
        for side in range(2):
            mine = (lane // HD) == side
            prob = prob_ref[0, 2 * pair + side]
            dprob = dot(jnp.where(mine, grad, jnp.zeros_like(grad)), value, NT)
            wide = prob.astype(F32)
            both = wide * dprob
            dscore = both - wide * jnp.sum(both, axis=1, keepdims=True)
            dbias_ref[2 * pair + side] += dscore
            draw = (dscore * HD**-0.5).astype(BF)
            queries.append(dot(draw, key))
            keys.append(dot(draw, query, TN))
            values.append(dot(prob, grad, TN))
        for place, pieces in enumerate((queries, keys, values)):
            at = place * D + lo
            dqkv_ref[:, at : at + 2 * HD] = jnp.where(lane < HD, pieces[0], pieces[1]).astype(BF)


def attend_back(qkv, prob, grad):
    count = qkv.shape[0] // TOK
    return pl.pallas_call(
        attend_back_kernel,
        grid=(count,),
        out_shape=(
            jax.ShapeDtypeStruct((count * TOK, 3 * D), BF),
            jax.ShapeDtypeStruct((H, TOK, TOK), F32),
        ),
        in_specs=[
            pl.BlockSpec((TOK, 3 * D), lambda i: (i, 0)),
            pl.BlockSpec((1, H, TOK, TOK), lambda i: (i, 0, 0, 0)),
            pl.BlockSpec((TOK, D), lambda i: (i, 0)),
        ],
        out_specs=(
            pl.BlockSpec((TOK, 3 * D), lambda i: (i, 0)),
            pl.BlockSpec((H, TOK, TOK), lambda i: (0, 0, 0)),
        ),
        compiler_params=pltpu.CompilerParams(vmem_limit_bytes=48 << 20),
    )(qkv, prob, grad)


def normal_parts(values):
    centered = values - jnp.mean(values, axis=-1, keepdims=True)
    spread = jnp.mean(centered * centered, axis=-1, keepdims=True)
    scale = lax.rsqrt(spread + norm_eps)
    return centered * scale, scale


def layer_norm(values, gain_row, bias_row):
    return (normal_parts(values)[0] * gain_row + bias_row).astype(BF)


def layer_norm_back(values, gain_row, grad):
    normal, scale = normal_parts(values)
    inner = grad * gain_row
    mean_one = jnp.mean(inner, axis=-1, keepdims=True)
    mean_two = jnp.mean(inner * normal, axis=-1, keepdims=True)
    back = (inner - mean_one - normal * mean_two) * scale
    return back, jnp.sum(grad * normal, axis=0), jnp.sum(grad, axis=0)


def unpack(vectors):
    pieces = [vectors[slot * D : (slot + 1) * D] for slot in range(10)]
    fc_bias = vectors[10 * D : 10 * D + FF]
    bias_table = vectors[10 * D + FF :].reshape(H, NREL)
    return (pieces, fc_bias, bias_table)


def layer_forward(states, full, vectors, bias):
    qkv_full, out_full, up_full, down_full = full
    pieces, fc_bias, unused = unpack(vectors)
    (gain_one, bias_one, query_bias, value_bias, out_bias) = pieces[:5]
    (scale_one, gain_two, bias_two, down_bias, scale_two) = pieces[5:]
    qkv_bias = jnp.concatenate([query_bias, jnp.zeros_like(query_bias), value_bias])
    normed = layer_norm(states, gain_one, bias_one)
    qkv = (dot(normed, qkv_full, NT) + qkv_bias).astype(BF)
    attended, prob = attend(qkv, bias)
    first = dot(attended, out_full, NT) + out_bias
    mid = states + scale_one * first
    normed_two = layer_norm(mid, gain_two, bias_two)
    raised = dot(normed_two, up_full, NT) + fc_bias
    below = 0.5 + 0.5 * lax.erf(raised * 0.5**0.5)
    hidden = (raised * below).astype(BF)
    slope = (below + raised * jnp.exp(-0.5 * raised * raised) * 0.3989422804014327).astype(BF)
    second = dot(hidden, down_full) + down_bias
    kept = (states, normed, qkv, prob, attended, first.astype(BF), mid, normed_two)
    return mid + scale_two * second, kept + (hidden, slope, second.astype(BF))


def layer_back(grad, kept, full, vectors):
    states, normed, qkv, prob, attended, first, mid, normed_two, hidden, slope, second = kept
    qkv_full, out_full, up_full, down_full = full
    pieces, unused, unused_table = unpack(vectors)
    gain_one, scale_one, gain_two, scale_two = (pieces[0], pieces[5], pieces[6], pieces[9])
    dsecond = (grad * scale_two).astype(BF)
    dscale_two = jnp.sum(grad * second.astype(F32), axis=0)
    ddown_bias = jnp.sum(dsecond.astype(F32), axis=0)
    ddown = dot(hidden, dsecond, TN).astype(BF)
    draised = (dot(dsecond, down_full, NT) * slope.astype(F32)).astype(BF)
    dfc_bias = jnp.sum(draised.astype(F32), axis=0)
    dup = dot(draised, normed_two, TN).astype(BF)
    back, dgain_two, dbias_two = layer_norm_back(mid, gain_two, dot(draised, up_full))
    dmid = grad + back
    dfirst = (dmid * scale_one).astype(BF)
    dscale_one = jnp.sum(dmid * first.astype(F32), axis=0)
    dout_bias = jnp.sum(dfirst.astype(F32), axis=0)
    dout = dot(dfirst, attended, TN).astype(BF)
    dattended = dot(dfirst, out_full).astype(BF)
    dqkv, dbias = attend_back(qkv, prob, dattended)
    dtable = reduce_bias(dbias)
    dqkv_bias = jnp.sum(dqkv.astype(F32), axis=0)
    dqkv_weight = dot(dqkv, normed, TN).astype(BF)
    back, dgain_one, dbias_one = layer_norm_back(states, gain_one, dot(dqkv, qkv_full))
    pieces = [
        dgain_one,
        dbias_one,
        dqkv_bias[:D],
        dqkv_bias[2 * D :],
        dout_bias,
        dscale_one,
        dgain_two,
        dbias_two,
        ddown_bias,
        dscale_two,
        dfc_bias,
        dtable.reshape(-1),
    ]
    return dmid + back, (dqkv_weight, dout, dup, ddown), jnp.concatenate(pieces)


def adam_parts(grad, first_moment, second_moment):
    first_moment = beta_one * first_moment + (1 - beta_one) * grad
    second_moment = beta_two * second_moment + (1 - beta_two) * grad * grad
    update = (
        first_moment
        / (1 - beta_one**STEP)
        / (jnp.sqrt(second_moment / (1 - beta_two**STEP)) + adam_eps)
    )
    return update, first_moment, second_moment


def adam_step(weight, grad, first_moment, second_moment, decay, rate):
    update, first_moment, second_moment = adam_parts(grad, first_moment, second_moment)
    return (weight - rate * (update + decay * weight), first_moment, second_moment)


def product(left_side, right_side, dims=NN):
    return lax.dot_general(
        left_side, right_side, dims, precision=lax.Precision.HIGH, preferred_element_type=F32
    )


def gather_weights(shards):
    return [lax.all_gather(shard, "fsdp", axis=0, tiled=True) for shard in shards]


def gather_rows(rows):
    return lax.all_gather(rows, "fsdp", axis=0, tiled=True)


def gather_stats(stats):
    return lax.all_gather(stats, "fsdp")


def scatter_rows(grads):
    return lax.psum_scatter(grads, "fsdp", scatter_dimension=0, tiled=True).astype(F32)


def reduce_weights(grads):
    scattered = [
        lax.psum_scatter(grad, "fsdp", scatter_dimension=0, tiled=True) for grad in grads
    ]
    return [lax.psum(part, "grp").astype(F32) for part in scattered]


def body(
    patches,
    positions,
    codes,
    owners,
    bases,
    patch_weight,
    head_weight,
    vocab_bias,
    token_vectors,
    qkv_weight,
    out_weight,
    up_weight,
    down_weight,
    layer_vectors,
    first_patch,
    first_head,
    first_vocab,
    first_token,
    first_qkv,
    first_out,
    first_up,
    first_down,
    first_layer,
    second_patch,
    second_head,
    second_vocab,
    second_token,
    second_qkv,
    second_out,
    second_up,
    second_down,
    second_layer,
):
    layers = qkv_weight.shape[0]
    count = patches.shape[0]
    tokens = count * TOK
    picked = count * NMASK
    row_count = -(-picked // 16) * 16
    vocab_local = head_weight.shape[1]
    place = lax.axis_index("fsdp")
    vocab_ids = place * vocab_local + jnp.arange(vocab_local, dtype=jnp.int32)

    shards = [patch_weight.T.astype(BF)]
    for index in range(layers):
        shards += [
            qkv_weight[index].T.astype(BF),
            out_weight[index].T.astype(BF),
            up_weight[index].T.astype(BF),
            down_weight[index].astype(BF),
        ]
    gathered = gather_weights(shards)
    patch_full = gathered[0]
    full = [gathered[1 + 4 * index : 5 + 4 * index] for index in range(layers)]
    biases = [expand_bias(unpack(layer_vectors[index])[2]) for index in range(layers)]

    flat_patches = jnp.pad(patches, ((0, 0), (0, TOK - NPATCH), (0, 0))).reshape(tokens, D)
    slots = jnp.arange(TOK, dtype=jnp.int32)
    hit = (positions[:, :, None] - 1 == slots[None, None, :]).astype(F32)
    masked = jnp.sum(hit, axis=1).reshape(tokens, 1)
    slot_of = jnp.tile(slots, count)[:, None]
    is_patch = (slot_of < NPATCH).astype(F32)
    is_class = (slot_of == NPATCH).astype(F32)
    shown = is_patch * (1.0 - masked)
    states = (dot(flat_patches, patch_full, NT) + token_vectors[0]) * shown
    states = states + token_vectors[2] * masked + token_vectors[1] * is_class

    kept = []
    for index in range(layers):
        states, saved = layer_forward(states, full[index], layer_vectors[index], biases[index])
        kept.append(saved)

    flat_positions = (positions - 1 + TOK * jnp.arange(count, dtype=jnp.int32)[:, None]).reshape(-1)
    flat_positions = jnp.pad(flat_positions, (0, row_count - picked), constant_values=-1)
    select = (flat_positions[:, None] == jnp.arange(tokens, dtype=jnp.int32)[None, :]).astype(BF)
    rows = dot(select, layer_norm(states, token_vectors[3], token_vectors[4])).astype(BF)

    all_rows = gather_rows(rows)
    flat_codes = jnp.pad(codes.reshape(-1), (0, row_count - picked), constant_values=-1)
    all_codes = gather_rows(flat_codes)
    head_low = head_weight.astype(BF)
    logits = dot(all_rows, head_low) + vocab_bias
    local_max = jnp.max(logits, axis=1)
    local_sum = jnp.sum(jnp.exp(logits - local_max[:, None]), axis=1)
    hits = all_codes[:, None] == vocab_ids[None, :]
    local_target = jnp.sum(jnp.where(hits, logits, 0.0), axis=1)
    stats = gather_stats(jnp.stack([local_max, local_sum, local_target]))
    top = jnp.max(stats[:, 0], axis=0)
    total = jnp.sum(stats[:, 1] * jnp.exp(stats[:, 0] - top), axis=0)
    target = jnp.sum(stats[:, 2], axis=0)
    log_total = top + jnp.log(total)
    valid = all_codes >= 0
    row_loss = jnp.where(valid, log_total - target, 0.0)
    loss_sum = jnp.sum(lax.dynamic_slice_in_dim(row_loss, place * row_count, row_count))
    logit_grads = jnp.exp(logits - log_total[:, None]) - hits.astype(F32)
    logit_grads = jnp.where(valid[:, None], logit_grads, 0.0)
    rounded = logit_grads.astype(BF)
    grad_head = dot(all_rows, rounded, TN)
    grad_vocab = jnp.sum(logit_grads, axis=0)
    row_grads = scatter_rows(dot(rounded, head_low, NT).astype(BF))

    high, middle, unused = three_parts(row_grads)
    dnormed = dot(select, high, TN) + dot(select, middle, TN)
    back, dgain, dbias = layer_norm_back(states, token_vectors[3], dnormed)
    deltas = [None] * layers
    grad_layers = [None] * layers
    for index in reversed(range(layers)):
        back, deltas[index], grad_layers[index] = layer_back(
            back, kept[index], full[index], layer_vectors[index]
        )
    dpatch = (back * shown).astype(BF)
    grad_token = jnp.stack(
        [
            jnp.sum(dpatch.astype(F32), axis=0),
            jnp.sum(back * is_class, axis=0),
            jnp.sum(back * masked, axis=0),
            dgain,
            dbias,
        ]
    )
    delta_patch = dot(dpatch, flat_patches, TN).astype(BF)
    grad_layer = jnp.stack(grad_layers)

    reduced = reduce_weights([delta_patch] + [item for delta in deltas for item in delta])
    grad_head = lax.psum(grad_head.astype(BF), "grp").astype(F32)
    grad_vocab = lax.psum(grad_vocab, "grp")
    grad_token, grad_layer, loss_sum = lax.psum((grad_token, grad_layer, loss_sum), ("grp", "fsdp"))
    sharded_squares = jnp.zeros((), F32)
    for grad in reduced + [grad_head, grad_vocab]:
        sharded_squares = sharded_squares + jnp.sum(grad * grad)
    replicated_squares = jnp.sum(grad_token * grad_token) + jnp.sum(grad_layer * grad_layer)
    squares = lax.psum(sharded_squares + replicated_squares / lax.axis_size("fsdp"), "fsdp")
    clip_norm = jnp.sqrt(squares)
    clip_scale = jnp.minimum(1.0, clip_level / (clip_norm + 1e-06))
    updates = [
        adam_step(
            patch_weight,
            reduced[0].T * clip_scale,
            first_patch,
            second_patch,
            weight_decay,
            matrix_rate,
        ),
        adam_step(
            head_weight, grad_head * clip_scale, first_head, second_head, weight_decay, matrix_rate
        ),
        adam_step(vocab_bias, grad_vocab * clip_scale, first_vocab, second_vocab, 0.0, vector_rate),
        adam_step(
            token_vectors, grad_token * clip_scale, first_token, second_token, 0.0, vector_rate
        ),
    ]
    matrices = [
        (qkv_weight, first_qkv, second_qkv),
        (out_weight, first_out, second_out),
        (up_weight, first_up, second_up),
        (down_weight, first_down, second_down),
    ]
    for kind in range(4):
        weight_all, moment_all, square_all = matrices[kind]
        results = []
        for index in range(layers):
            basis = bases[4 * index + kind]
            grad = reduced[1 + 4 * index + kind]
            if kind < 3:
                turned = product(basis, grad, (((0,), (1,)), ((), ())))
            else:
                turned = product(grad, basis)
            update, moment, square = adam_parts(
                turned * clip_scale, moment_all[index], square_all[index]
            )
            update = product(basis, update) if kind < 3 else product(update, basis, NT)
            weight = weight_all[index]
            results.append(
                (weight - matrix_rate * (update + weight_decay * weight), moment, square)
            )
        updates.append(
            tuple((jnp.stack([result[member] for result in results]) for member in range(3)))
        )
    updates.append(
        adam_step(
            layer_vectors, grad_layer * clip_scale, first_layer, second_layer, 0.0, vector_rate
        )
    )
    return (
        loss_sum,
        clip_norm,
        *[entry[0] for entry in updates],
        *[entry[1] for entry in updates],
        *[entry[2] for entry in updates],
    )


def solution(mesh):
    weights = (
        P(None, "fsdp"),
        P(None, "fsdp"),
        P("fsdp"),
        P(),
        P(None, None, "fsdp"),
        P(None, None, "fsdp"),
        P(None, None, "fsdp"),
        P(None, "fsdp", None),
        P(),
    )
    placed = (
        P(("grp", "fsdp"), None, None),
        P(("grp", "fsdp"), None),
        P(("grp", "fsdp"), None),
        P(),
        P(),
        *weights,
        *weights,
        *weights,
    )
    return jax.shard_map(
        body,
        mesh=mesh,
        in_specs=placed,
        out_specs=(P(), P(), *weights, *weights, *weights),
        check_vma=False,
    )
```
